32 devices in a mesh: row: 16 (over z, y, x), col: 2 (over core).
Axes of the slice: x: 2, y: 2, z: 4, core: 2. Of those that a mesh axis runs over, the one named last changes fastest.
Arguments:
- panel: float32 [8192, 2048], P('row', 'col'), may hold values from -6 to 6
- inner_vecs: float32 [16, 4, 256, 128], P('row', None, 'col'), may hold values from -0.375 to 0.375
- inner_factor: float32 [16, 4, 128, 128], P('row'), may hold values from -0.5 to 0.5
- border_vecs: float32 [16, 4, 256, 128], P('row', None, 'col'), may hold values from -0.375 to 0.375
- border_factor: float32 [16, 4, 128, 128], P('row'), may hold values from -0.5 to 0.5
- group_start: int32 [4], replicated, may hold values from 0 to 12
- group_span: int32 [4], replicated, may hold values from 3 to 15
Outputs:
- panel_out: float32 [8192, 2048], P('row', 'col')
The draws below stay inside these ranges and needn't reach their ends.
All inputs are finite; a program needn't handle non-finite values.
Results may differ from the reference program's by a relative error of at most 0.00011.
Values sent between devices are 32-bit elements; how exact they have to be, the bound alone decides.
No kernel may reach another device: no remote copies, remote signals or barrier semaphores. Data moves between devices by JAX's collectives and lax.ppermute only.
A program may use at most 64 MiB of HBM per device.

```python
import jax
import jax.numpy as jnp
from jax import lax

NB = 128
BAND = 256
ROWS_DEV = 512
STEPS = 4
ORDER = 8192
NVEC = 2048
N_ROW = 16


def group_draw(key):
    key = jax.random.fold_in(key, 11)
    limit = N_ROW - 1
    keys = jax.random.split(key, 2 * STEPS)
    lowest = max(limit // 4, 1)
    current = jnp.array(limit, jnp.int32)
    spans = [current]
    for index in range(1, STEPS):
        if index == STEPS - 1:
            current = jnp.array(lowest, jnp.int32)
        else:
            current = jax.random.randint(keys[index], (), lowest, current + 1, dtype=jnp.int32)
        spans.append(current)
    starts = []
    for index in range(STEPS):
        if index == STEPS - 1:
            starts.append(jnp.array(limit - lowest, jnp.int32))
        else:
            starts.append(jax.random.randint(keys[STEPS + index], (), 0, limit - spans[index] + 1, dtype=jnp.int32))
    return (jnp.stack(starts).astype(jnp.int32), jnp.stack(spans).astype(jnp.int32))


def draw_group_start(key, part):
    return group_draw(key)[0]


def draw_group_span(key, part):
    return group_draw(key)[1]


def level_of(rng, extent, pieces, smallest, high):
    loudness = 1.0
    for axis_at, parts in pieces:
        draws = jax.random.uniform(jax.random.fold_in(jax.random.fold_in(rng, 6), axis_at), (parts,), jnp.float32, smallest / len(pieces), high / len(pieces))
        loudness = loudness * jnp.repeat(jnp.exp(draws), extent[axis_at] // parts).reshape((-1,) + (1,) * (len(extent) - 1 - axis_at))
    return loudness


def bell_draw(rng, shape, spread, most, cuts=(), kind=jnp.bfloat16):
    factor_of = level_of(rng, shape, cuts, -0.22, 0.18) if cuts else 1.0
    result = jax.random.normal(rng, shape, jnp.float32) * spread * factor_of
    return jnp.minimum(jnp.maximum(result, -most), most).astype(kind)


def setup_inputs(seed: int = 0) -> dict:
    key_of = jax.random.split(jax.random.key(seed), 8)
    panel = bell_draw(key_of[0], (ORDER, NVEC), 1.0, 6.0, ((0, 16), (1, 2)), jnp.float32)
    inner_vecs = bell_draw(key_of[1], (N_ROW, STEPS, BAND, NB), BAND ** -0.5, 0.375, ((0, 16), (2, 2)), jnp.float32)
    inner_factor = bell_draw(key_of[2], (N_ROW, STEPS, NB, NB), NB ** -0.5, 0.5, ((0, 16),), jnp.float32)
    border_vecs = bell_draw(key_of[3], (N_ROW, STEPS, BAND, NB), BAND ** -0.5, 0.375, ((0, 16), (2, 2)), jnp.float32)
    border_factor = bell_draw(key_of[4], (N_ROW, STEPS, NB, NB), NB ** -0.5, 0.5, ((0, 16),), jnp.float32)
    group_start = draw_group_start(jax.random.fold_in(key_of[7], 71), 0)
    group_span = draw_group_span(jax.random.fold_in(key_of[7], 71), 0)
    return dict(panel=panel, inner_vecs=inner_vecs, inner_factor=inner_factor, border_vecs=border_vecs, border_factor=border_factor, group_start=group_start, group_span=group_span)


def reflect(vectors, factor, band):
    inner = jnp.einsum("nbk,nbc->nkc", vectors, band, precision=lax.Precision.HIGHEST)
    scaled = jnp.einsum("nkj,njc->nkc", factor, inner, precision=lax.Precision.HIGHEST)
    return jnp.einsum("nbk,nkc->nbc", vectors, scaled, precision=lax.Precision.HIGHEST)


def reference(panel, inner_vecs, inner_factor, border_vecs, border_factor, group_start, group_span):
    sections = panel.reshape(N_ROW, ROWS_DEV, NVEC)
    section_ids = jnp.arange(N_ROW, dtype=jnp.int32)
    for step in range(STEPS):
        active = (section_ids >= group_start[step]) & (section_ids < group_start[step] + group_span[step])
        if step % 2 == 0:
            middle = sections[:, NB:3 * NB]
            sections = sections.at[:, NB:3 * NB].set(middle - reflect(inner_vecs[:, step], inner_factor[:, step], middle))
            band = jnp.concatenate([sections[:-1, ROWS_DEV - NB:], sections[1:, :NB]], axis=1)
            change = reflect(border_vecs[:-1, step], border_factor[:-1, step], band)
            change = jnp.where(active[:-1, None, None], change, jnp.zeros_like(change))
            sections = sections.at[:-1, ROWS_DEV - NB:].set(sections[:-1, ROWS_DEV - NB:] - change[:, :NB])
            sections = sections.at[1:, :NB].set(sections[1:, :NB] - change[:, NB:])
        else:
            upper = sections[:, :2 * NB]
            sections = sections.at[:, :2 * NB].set(upper - reflect(inner_vecs[:, step], inner_factor[:, step], upper))
            lower = sections[:, 2 * NB:]
            change = reflect(border_vecs[:, step], border_factor[:, step], lower)
            change = jnp.where(active[:, None, None], change, jnp.zeros_like(change))
            sections = sections.at[:, 2 * NB:].set(lower - change)
    return sections.reshape(ORDER, NVEC)
```

```python
import jax
import jax.numpy as jnp
from jax import lax
from jax.experimental import pallas as pl
from jax.experimental.pallas import tpu as pltpu
from jax.sharding import PartitionSpec as P

F32 = jnp.float32
TILES = 4
VMEM_LIMIT = 24 * 1024 * 1024


def from_behind(value, axis, by):
    devices = lax.axis_size(axis)
    pairs = [(i, i + by) for i in range(devices) if 0 <= i + by < devices]
    return lax.ppermute(value, axis, pairs)


def other_core(value):
    cores = lax.axis_size("col")
    return lax.ppermute(value, "col", [(i, (i + 1) % cores) for i in range(cores)])


def exact_dot(x, y, contract=(1, 0)):
    return lax.dot_general(
        x,
        y,
        (((contract[0],), (contract[1],)), ((), ())),
        precision=lax.Precision.HIGHEST,
        preferred_element_type=F32,
    )


def split(x):
    high = x.astype(jnp.bfloat16)
    return high, (x - high.astype(F32)).astype(jnp.bfloat16)


def dot(x, y):
    xh, xl = split(x)
    yh, yl = split(y)
    small = jnp.dot(xl, yh, preferred_element_type=F32) + jnp.dot(
        xh, yl, preferred_element_type=F32
    )
    return small + jnp.dot(xh, yh, preferred_element_type=F32)


def change_of(first, second, factor, core):
    upper = jnp.where(core == 0, first, second)
    lower = jnp.where(core == 0, second, first)
    vectors = jnp.concatenate([upper, lower], axis=0)
    return exact_dot(exact_dot(vectors, factor), vectors, (1, 1))


def stacked(upper, lower):
    return jnp.concatenate([upper, lower], axis=0)


def is_active(flags, step):
    return flags[step] != 0


def first_kernel(flags, own, other, factor, b, c, early, bc, message):
    tile = pl.program_id(0)
    width = factor.shape[-1]

    @pl.when(tile == 0)
    def _():
        core = flags[5]
        for step in range(2):
            early[step] = change_of(own[step], other[step], factor[step], core)

    band = stacked(b[...], c[...])
    band = band - dot(early[0], band)
    bc[...] = band
    message[:width] = dot(early[1, :width, width:], band[:width])
    span = message.shape[1]
    for block in range(span // width):
        message[width:, block * width : (block + 1) * width] = early[
            1, pl.ds((tile * (span // width) + block) * (message.shape[0] - width), message.shape[0] - width), :width
        ]


def matrix_kernel(flags, own_i, other_i, fac_i, own_b, other_b, fac_b, late, border):
    core = flags[5]
    for step in range(late.shape[0]):
        late[step] = change_of(own_i[step + 2], other_i[step + 2], fac_i[step + 2], core)
    for step in range(border.shape[0]):
        border[step] = change_of(own_b[step], other_b[step], fac_b[step], core)


def second_kernel(flags, d, below, c, border, message, cd):
    width = d.shape[0]
    band = stacked(d[...], below[...])
    band = jnp.where(is_active(flags, 0), band - dot(border[0], band), band)
    message[...] = band[width:]
    band = stacked(c[...], band[:width])
    cd[...] = jnp.where(is_active(flags, 1), band - dot(border[1], band), band)


def third_kernel(flags, below, message, mixing, d, border, sent, d_out):
    width = d.shape[0]
    span = message.shape[1]
    low = below[...]
    low = low - dot(mixing[...], low) - message[...]
    band = stacked(d[...], low)
    band = jnp.where(is_active(flags, 2), band - dot(border[0], band), band)
    d_out[...] = band[:width]
    sent[...] = band[width:]


def fourth_kernel(flags, raw, above, b, c, d, second, late, border, out):
    width = raw.shape[0]
    first = flags[4] != 0
    ab = stacked(jnp.where(first, raw[...], above[...]), b[...])
    ab = ab - dot(second[0], ab)
    bc = stacked(ab[width:], c[...])
    bc = bc - dot(late[0], bc)
    cd = stacked(bc[width:], d[...])
    out[2 * width :] = jnp.where(is_active(flags, 3), cd - dot(border[0], cd), cd)
    ab = stacked(jnp.where(first, ab[:width], 0.0), bc[:width])
    out[: 2 * width] = ab - dot(late[1], ab)


def last_kernel(above, late, before, out):
    width = above.shape[0]
    top = above[...]
    change = dot(late[0], top)
    out[:width] = before[:width] + (top - change[:width])
    out[width:] = before[width:] - change[width:]


def smem():
    return pl.BlockSpec(memory_space=pltpu.SMEM)


def whole(shape, index=None):
    index = (0,) * len(shape) if index is None else index
    return pl.BlockSpec(shape, lambda tile: index)


def columns(rows, span, row=0):
    return pl.BlockSpec((rows, span), lambda tile: (row, tile))


def call(kernel, tiles, in_specs, out_specs, out_shape, operands, flops, name, **extra):
    shapes = [jax.ShapeDtypeStruct(shape, F32) for shape in out_shape]
    size = sum(4 * o.size for o in operands) + sum(4 * s.size for s in shapes)
    return pl.pallas_call(
        kernel,
        grid=(tiles,),
        in_specs=in_specs,
        out_specs=out_specs,
        out_shape=shapes,
        cost_estimate=pl.CostEstimate(
            flops=int(flops), bytes_accessed=int(size), transcendentals=0
        ),
        compiler_params=pltpu.CompilerParams(vmem_limit_bytes=VMEM_LIMIT),
        name=name,
        **extra,
    )(*operands)


def local(panel, inner_vecs, inner_factor, border_vecs, border_factor, group_start, group_span):
    width = inner_factor.shape[-1]
    height, cols = panel.shape
    steps = inner_factor.shape[1]
    span = cols // TILES
    index = lax.axis_index("row")
    core = lax.axis_index("col")
    active = (index >= group_start) & (index < group_start + group_span)
    flags = jnp.concatenate(
        [
            active.astype(jnp.int32),
            jnp.stack([(index == 0).astype(jnp.int32), core.astype(jnp.int32)]),
        ]
    )
    own_i, own_b = inner_vecs[0], border_vecs[0]
    fac_i, fac_b = inner_factor[0], border_factor[0]

    below = from_behind(panel[:width], "row", -1)
    other_i = other_core(own_i)
    other_b = other_core(own_b)

    square = (2 * width, 2 * width)
    vec = (steps, width, width)
    extra = width * width // cols
    unit = 2 * width * width * cols * 3
    early, bc, up_message = call(
        first_kernel,
        TILES,
        [smem(), whole(vec), whole(vec), whole(vec), columns(width, span, 1), columns(width, span, 2)],
        [whole((2,) + square), columns(2 * width, span), columns(width + extra, span)],
        [(2,) + square, (2 * width, cols), (width + extra, cols)],
        [flags, own_i, other_i, fac_i, panel, panel],
        5 * unit,
        "inner_and_up",
    )
    from_below = from_behind(up_message, "row", -1)
    late, border = call(
        matrix_kernel,
        1,
        [smem()] + [whole(vec)] * 6,
        [whole((2,) + square), whole((steps,) + square)],
        [(2,) + square, (steps,) + square],
        [flags, own_i, other_i, fac_i, own_b, other_b, fac_b],
        6 * unit,
        "matrices",
    )
    down_message, cd = call(
        second_kernel,
        TILES,
        [smem(), columns(width, span, 3), columns(width, span), columns(width, span, 1), whole((2,) + square)],
        [columns(width, span), columns(2 * width, span)],
        [(width, cols), (2 * width, cols)],
        [flags, panel, below, bc, border],
        8 * unit,
        "border_and_down",
    )
    above = from_behind(down_message, "row", 1)
    mixing = from_below[width:].reshape(extra, cols // width, width)
    mixing = mixing.transpose(1, 0, 2).reshape(width, width)
    sent, d = call(
        third_kernel,
        TILES,
        [smem(), columns(width, span), columns(width, span), whole((width, width)), columns(width, span, 1), whole((1,) + square, (2, 0, 0))],
        [columns(width, span), columns(width, span)],
        [(width, cols), (width, cols)],
        [flags, down_message, from_below, mixing, cd, border],
        5 * unit,
        "second_border",
    )
    last = from_behind(sent, "row", 1)
    (out,) = call(
        fourth_kernel,
        TILES,
        [smem(), columns(width, span), columns(width, span), columns(width, span), columns(width, span), columns(width, span), whole((1,) + square, (1, 0, 0)), whole((2,) + square), whole((1,) + square, (3, 0, 0))],
        [columns(height, span)],
        [(height, cols)],
        [flags, panel, above, bc, cd, d, early, late, border],
        16 * unit,
        "rest",
    )
    (out,) = call(
        last_kernel,
        TILES,
        [columns(width, span), whole((1, 2 * width, width), (1, 0, 0)), columns(2 * width, span)],
        [columns(2 * width, span)],
        [(height, cols)],
        [last, late, out],
        2 * unit,
        "finish",
        input_output_aliases={2: 0},
    )
    return out


def solution(mesh):
    placed = (
        P("row", "col"),
        P("row", None, "col", None),
        P("row", None, None, None),
        P("row", None, "col", None),
        P("row", None, None, None),
        P(),
        P(),
    )
    return jax.shard_map(
        local, mesh=mesh, in_specs=placed, out_specs=P("row", "col"), check_vma=False
    )
```

```python
import functools

import jax
import jax.numpy as jnp
from jax import lax
from jax.experimental import pallas as pl
from jax.experimental.pallas import tpu as pltpu
from jax.sharding import PartitionSpec as P

F32 = jnp.float32
TILES = 2
EIGHTHS_UP = (4, 4)
EIGHTHS_DOWN = (4, 4)
VMEM_LIMIT = 24 * 1024 * 1024


def from_behind(value, axis, by):
    devices = lax.axis_size(axis)
    pairs = [(i, i + by) for i in range(devices) if 0 <= i + by < devices]
    return lax.ppermute(value, axis, pairs)


def other_core(value):
    cores = lax.axis_size("col")
    return lax.ppermute(value, "col", [(i, (i + 1) % cores) for i in range(cores)])


def split(x):
    high = x.astype(jnp.bfloat16)
    return high, (x - high.astype(F32)).astype(jnp.bfloat16)


def dot(x, y, contract=(1, 0)):
    def product(left, right):
        return lax.dot_general(
            left,
            right,
            (((contract[0],), (contract[1],)), ((), ())),
            preferred_element_type=F32,
        )

    xh, xl = split(x)
    yh, yl = split(y)
    return product(xl, yh) + product(xh, yl) + product(xh, yh)


def change_of(first, second, factor, core):
    upper = jnp.where(core == 0, first, second)
    lower = jnp.where(core == 0, second, first)
    vectors = jnp.concatenate([upper, lower], axis=0)
    return dot(dot(vectors, factor), vectors, (1, 1))


def stacked(upper, lower):
    return jnp.concatenate([upper, lower], axis=0)


def is_active(starts, spans, step):
    index = lax.axis_index("row")
    return (index >= starts[step]) & (index < starts[step] + spans[step])


def pieces(cols, eighths):
    ends = [cols * sum(eighths[:at]) // 8 for at in range(len(eighths) + 1)]
    return [slice(a, b) for a, b in zip(ends[:-1], ends[1:])]


def first_kernel(own, other, factor, panel, early, bc, *rest):
    *messages, vectors, factors, band, sems = rest
    width = factor.shape[-1]
    parts = pieces(panel.shape[1], EIGHTHS_UP)
    copies = [
        pltpu.make_async_copy(own.at[pl.ds(0, 2)], vectors, sems.at[0]),
        pltpu.make_async_copy(factor.at[pl.ds(0, 2)], factors, sems.at[1]),
    ] + [
        pltpu.make_async_copy(
            panel.at[pl.ds(width, 2 * width), part], band.at[:, part], sems.at[2 + at]
        )
        for at, part in enumerate(parts)
    ]
    for copy in copies:
        copy.start()
    copies[0].wait()
    copies[1].wait()
    core = lax.axis_index("col")
    for step in range(2):
        early[step] = change_of(vectors[step], other[step], factors[step], core)
    last = messages[-1]
    extra = last.shape[0] - width
    for block in range(last.shape[1] // width):
        last[width:, block * width : (block + 1) * width] = early[
            1, block * extra : (block + 1) * extra, :width
        ]
    for at, part in enumerate(parts):
        copies[2 + at].wait()
        tall = band[:, part]
        tall = tall - dot(early[0], tall)
        bc[:, part] = tall
        messages[at][:width] = dot(early[1, :width, width:], tall[:width])


def matrix_kernel(own_i, other_i, fac_i, own_b, other_b, fac_b, late, border):
    core = lax.axis_index("col")
    for step in range(late.shape[0]):
        late[step] = change_of(own_i[step], other_i[step], fac_i[step], core)
    for step in range(border.shape[0]):
        border[step] = change_of(own_b[step], other_b[step], fac_b[step], core)


def second_kernel(starts, spans, d, below, c, border, message, cd):
    width = d.shape[0]
    band = stacked(d[...], below[...])
    band = jnp.where(is_active(starts, spans, 0), band - dot(border[0], band), band)
    message[...] = band[width:]
    band = stacked(c[...], band[:width])
    cd[...] = jnp.where(is_active(starts, spans, 1), band - dot(border[1], band), band)


def third_kernel(starts, spans, below, cd, border, *rest):
    count = len(EIGHTHS_UP)
    messages, d_out, sent = rest[:count], rest[count], rest[count + 1 :]
    width, cols = d_out.shape
    cuts = pieces(cols, EIGHTHS_DOWN)
    last = messages[-1]
    mixing = jnp.concatenate(
        [
            last[width:, block * width : (block + 1) * width]
            for block in range(last.shape[1] // width)
        ],
        axis=0,
    )
    for message, part in zip(messages, pieces(cols, EIGHTHS_UP)):
        low = below[:, part]
        low = low - dot(mixing, low) - message[:width]
        band = stacked(cd[width:, part], low)
        band = jnp.where(is_active(starts, spans, 2), band - dot(border[0], band), band)
        d_out[:, part] = band[:width]
        for cut, out in zip(cuts, sent):
            a, b = max(cut.start, part.start), min(cut.stop, part.stop)
            if a < b:
                out[:, a - cut.start : b - cut.start] = band[
                    width:, a - part.start : b - part.start
                ]


def fourth_kernel(starts, spans, raw, above, bc, cd, d, second, late, border, out, before, held, sems):
    width, cols = raw.shape
    span = cols // TILES
    first = lax.axis_index("row") == 0
    copies = []
    for part in range(TILES):
        here = slice(part * span, (part + 1) * span)
        ab = stacked(jnp.where(first, raw[:, here], above[:, here]), bc[:width, here])
        ab = ab - dot(second[0], ab)
        low = stacked(ab[width:], cd[:width, here])
        low = low - dot(late[0], low)
        end = stacked(low[width:], d[:, here])
        held[:, here] = jnp.where(is_active(starts, spans, 3), end - dot(border[0], end), end)
        copy = pltpu.make_async_copy(
            held.at[:, pl.ds(part * span, span)],
            out.at[pl.ds(2 * width, 2 * width), pl.ds(part * span, span)],
            sems.at[part],
        )
        copy.start()
        copies.append(copy)
        ab = stacked(jnp.where(first, ab[:width], 0.0), low[:width])
        before[:, here] = ab - dot(late[1], ab)
    for copy in copies:
        copy.wait()


def last_kernel(cut, above, late, before, out_in, out, held, sem):
    del out_in
    width = above.shape[0]
    top = above[...]
    change = dot(late[0], top)
    held[:width] = before[:width, cut] + (top - change[:width])
    held[width:] = before[width:, cut] - change[width:]
    copy = pltpu.make_async_copy(held, out.at[pl.ds(0, 2 * width), cut], sem)
    copy.start()
    copy.wait()


def smem():
    return pl.BlockSpec(memory_space=pltpu.SMEM)


def hbm():
    return pl.BlockSpec(memory_space=pltpu.HBM)


def whole(shape, index=None):
    index = (0,) * len(shape) if index is None else index
    return pl.BlockSpec(shape, lambda tile: index)


def columns(rows, span, row=0):
    return pl.BlockSpec((rows, span), lambda tile: (row, tile))


def call(kernel, tiles, in_specs, out_specs, out_shape, operands, name, vmem=VMEM_LIMIT, **extra):
    shapes = [jax.ShapeDtypeStruct(shape, F32) for shape in out_shape]
    return pl.pallas_call(
        kernel,
        grid=(tiles,),
        in_specs=in_specs,
        out_specs=out_specs,
        out_shape=shapes,
        cost_estimate=pl.CostEstimate(flops=1, bytes_accessed=1, transcendentals=0),
        compiler_params=pltpu.CompilerParams(vmem_limit_bytes=vmem),
        name=name,
        **extra,
    )(*operands)


def local(panel, inner_vecs, inner_factor, border_vecs, border_factor, group_start, group_span):
    width = inner_factor.shape[-1]
    height, cols = panel.shape
    steps = inner_factor.shape[1]
    span = cols // TILES
    own_i, own_b = inner_vecs[0], border_vecs[0]
    fac_i, fac_b = inner_factor[0], border_factor[0]

    below = from_behind(panel[:width], "row", -1)
    other_i = other_core(own_i)
    other_b = other_core(own_b)

    square = (2 * width, 2 * width)
    vec = (steps, width, width)
    ups = [part.stop - part.start for part in pieces(cols, EIGHTHS_UP)]
    cuts = pieces(cols, EIGHTHS_DOWN)
    downs = [cut.stop - cut.start for cut in cuts]
    extra = width * width // ups[-1]
    shapes = [(width, up) for up in ups[:-1]] + [(width + extra, ups[-1])]
    early, bc, *up_messages = call(
        first_kernel,
        1,
        [hbm(), whole((2, width, width)), hbm(), hbm()],
        [whole((2,) + square), whole((2 * width, cols))] + [whole(shape) for shape in shapes],
        [(2,) + square, (2 * width, cols)] + shapes,
        [own_i[:2], other_i, fac_i[:2], panel],
        "inner_and_up",
        vmem=50 * 1024 * 1024,
        scratch_shapes=[
            pltpu.VMEM((2, width, width), F32),
            pltpu.VMEM((2, width, width), F32),
            pltpu.VMEM((2 * width, cols), F32),
            pltpu.SemaphoreType.DMA((2 + len(ups),)),
        ],
    )
    from_below = [from_behind(message, "row", -1) for message in up_messages]
    below, from_below[0] = lax.optimization_barrier((below, from_below[0]))
    late, border = call(
        matrix_kernel,
        1,
        [whole((2, width, width), (1, 0, 0))] * 3 + [whole(vec)] * 3,
        [whole((2,) + square), whole((steps,) + square)],
        [(2,) + square, (steps,) + square],
        [own_i, other_i, fac_i, own_b, other_b, fac_b],
        "matrices",
    )
    down_message, cd = call(
        second_kernel,
        TILES,
        [smem(), smem(), columns(width, span, 3), columns(width, span), columns(width, span, 1), whole((2,) + square)],
        [columns(width, span), columns(2 * width, span)],
        [(width, cols), (2 * width, cols)],
        [group_start, group_span, panel, below, bc, border],
        "border_and_down",
    )
    above = from_behind(down_message, "row", 1)
    d, *sent = call(
        third_kernel,
        1,
        [smem(), smem(), whole((width, cols)), whole((2 * width, cols)), whole((1,) + square, (2, 0, 0))] + [whole(shape) for shape in shapes],
        [whole((width, cols))] + [whole((width, down)) for down in downs],
        [(width, cols)] + [(width, down) for down in downs],
        [group_start, group_span, down_message, cd, border] + from_below,
        "second_border",
    )
    last = [from_behind(part, "row", 1) for part in sent]
    out, before = call(
        fourth_kernel,
        1,
        [smem(), smem(), whole((width, cols)), whole((width, cols)), whole((2 * width, cols)), whole((2 * width, cols)), whole((width, cols)), whole((1,) + square, (1, 0, 0)), whole((2,) + square), whole((1,) + square, (3, 0, 0))],
        [pl.BlockSpec(memory_space=pl.ANY), whole((2 * width, cols))],
        [(height, cols), (2 * width, cols)],
        [group_start, group_span, panel, above, bc, cd, d, early, late, border],
        "rest",
        scratch_shapes=[pltpu.VMEM((2 * width, cols), F32), pltpu.SemaphoreType.DMA((TILES,))],
    )
    for cut, down, part in zip(cuts, downs, last):
        (out,) = call(
            functools.partial(last_kernel, cut),
            1,
            [whole((width, down)), whole((1, 2 * width, width), (1, 0, 0)), whole((2 * width, cols)), pl.BlockSpec(memory_space=pl.ANY)],
            [pl.BlockSpec(memory_space=pl.ANY)],
            [(height, cols)],
            [part, late, before, out],
            "finish",
            scratch_shapes=[pltpu.VMEM((2 * width, down), F32), pltpu.SemaphoreType.DMA],
            input_output_aliases={3: 0},
        )
    return out


def solution(mesh):
    placed = (
        P("row", "col"),
        P("row", None, "col", None),
        P("row", None, None, None),
        P("row", None, "col", None),
        P("row", None, None, None),
        P(),
        P(),
    )
    return jax.shard_map(
        local, mesh=mesh, in_specs=placed, out_specs=P("row", "col"), check_vma=False
    )
```

```python
import functools

import jax
import jax.numpy as jnp
from jax import lax
from jax.experimental import pallas as pl
from jax.experimental.pallas import tpu as pltpu
from jax.sharding import PartitionSpec as P

F32 = jnp.float32
TILES = 2
EIGHTHS_UP = (4, 4)
EIGHTHS_DOWN = (6, 2)
VMEM_LIMIT = 24 * 1024 * 1024


def from_behind(value, axis, by):
    devices = lax.axis_size(axis)
    pairs = [(i, i + by) for i in range(devices) if 0 <= i + by < devices]
    return lax.ppermute(value, axis, pairs)


def other_core(value):
    cores = lax.axis_size("col")
    return lax.ppermute(value, "col", [(i, (i + 1) % cores) for i in range(cores)])


def split(x):
    high = x.astype(jnp.bfloat16)
    return high, (x - high.astype(F32)).astype(jnp.bfloat16)


def dot(x, y, contract=(1, 0)):
    def product(left, right):
        return lax.dot_general(
            left,
            right,
            (((contract[0],), (contract[1],)), ((), ())),
            preferred_element_type=F32,
        )

    xh, xl = split(x)
    yh, yl = split(y)
    return product(xl, yh) + product(xh, yl) + product(xh, yh)


def change_of(first, second, factor, core):
    upper = jnp.where(core == 0, first, second)
    lower = jnp.where(core == 0, second, first)
    vectors = jnp.concatenate([upper, lower], axis=0)
    return dot(dot(vectors, factor), vectors, (1, 1))


def stacked(upper, lower):
    return jnp.concatenate([upper, lower], axis=0)


def unpacked(rows, width):
    return jnp.concatenate(
        [rows[:, at : at + width] for at in range(0, rows.shape[1], width)], axis=0
    )


def ordered(mine, other):
    core = lax.axis_index("col")
    return stacked(jnp.where(core == 0, mine, other), jnp.where(core == 0, other, mine))


def is_active(starts, spans, step):
    index = lax.axis_index("row")
    return (index >= starts[step]) & (index < starts[step] + spans[step])


def pieces(cols, eighths):
    ends = [cols * sum(eighths[:at]) // 8 for at in range(len(eighths) + 1)]
    return [slice(a, b) for a, b in zip(ends[:-1], ends[1:])]


def first_kernel(own, other, factor, panel, early, bc, *rest):
    *messages, vectors, factors, band, sems = rest
    width = factor.shape[-1]
    parts = pieces(panel.shape[1], EIGHTHS_UP)
    copies = [
        pltpu.make_async_copy(own.at[pl.ds(0, 2)], vectors, sems.at[0]),
        pltpu.make_async_copy(factor.at[pl.ds(0, 2)], factors, sems.at[1]),
    ] + [
        pltpu.make_async_copy(
            panel.at[pl.ds(width, 2 * width), part], band.at[:, part], sems.at[2 + at]
        )
        for at, part in enumerate(parts)
    ]
    for copy in copies:
        copy.start()
    copies[0].wait()
    copies[1].wait()
    core = lax.axis_index("col")
    for step in range(2):
        early[step] = change_of(vectors[step], other[step], factors[step], core)
    last = messages[-1]
    extra = last.shape[0] - width
    half = jnp.where(core == 0, early[1, : width // 2, :width], early[1, width // 2 : width, :width])
    for block in range(last.shape[1] // width):
        last[width:, block * width : (block + 1) * width] = half[
            block * extra : (block + 1) * extra
        ]
    for at, part in enumerate(parts):
        copies[2 + at].wait()
        tall = band[:, part]
        tall = tall - dot(early[0], tall)
        bc[:, part] = tall
        messages[at][:width] = dot(early[1, :width, width:], tall[:width])


def matrix_kernel(own_i, other_i, fac_i, own_b, other_b, fac_b, late, border):
    core = lax.axis_index("col")
    for step in range(late.shape[0]):
        late[step] = change_of(own_i[step], other_i[step], fac_i[step], core)
    for step in range(border.shape[0]):
        border[step] = change_of(own_b[step], other_b[step], fac_b[step], core)


def second_kernel(starts, spans, d, below, c, border, message, cd):
    width = d.shape[0]
    band = stacked(d[...], below[...])
    band = jnp.where(is_active(starts, spans, 0), band - dot(border[0], band), band)
    message[...] = band[width:]
    band = stacked(c[...], band[:width])
    cd[...] = jnp.where(is_active(starts, spans, 1), band - dot(border[1], band), band)


def third_kernel(starts, spans, below, cd, border, half, *rest):
    count = len(EIGHTHS_UP)
    messages, d_out, sent = rest[:count], rest[count], rest[count + 1 :]
    width, cols = d_out.shape
    cuts = pieces(cols, EIGHTHS_DOWN)
    mixing = ordered(unpacked(messages[-1][width:], width), unpacked(half[...], width))
    for message, part in zip(messages, pieces(cols, EIGHTHS_UP)):
        low = below[:, part]
        low = low - dot(mixing, low) - message[:width]
        band = stacked(cd[width:, part], low)
        band = jnp.where(is_active(starts, spans, 2), band - dot(border[0], band), band)
        d_out[:, part] = band[:width]
        for cut, out in zip(cuts, sent):
            a, b = max(cut.start, part.start), min(cut.stop, part.stop)
            if a < b:
                out[:, a - cut.start : b - cut.start] = band[
                    width:, a - part.start : b - part.start
                ]


def fourth_kernel(starts, spans, raw, above, bc, cd, d, second, late, border, out, *rest):
    *before, held, sems = rest
    width, cols = raw.shape
    span = cols // TILES
    first = lax.axis_index("row") == 0
    copies = []
    for part in range(TILES):
        here = slice(part * span, (part + 1) * span)
        ab = stacked(jnp.where(first, raw[:, here], above[:, here]), bc[:width, here])
        ab = ab - dot(second[0], ab)
        low = stacked(ab[width:], cd[:width, here])
        low = low - dot(late[0], low)
        end = stacked(low[width:], d[:, here])
        held[:, here] = jnp.where(is_active(starts, spans, 3), end - dot(border[0], end), end)
        copy = pltpu.make_async_copy(
            held.at[:, pl.ds(part * span, span)],
            out.at[pl.ds(2 * width, 2 * width), pl.ds(part * span, span)],
            sems.at[part],
        )
        copy.start()
        copies.append(copy)
        ab = stacked(jnp.where(first, ab[:width], 0.0), low[:width])
        ab = ab - dot(late[1], ab)
        for cut, kept in zip(pieces(cols, EIGHTHS_DOWN), before):
            a, b = max(cut.start, here.start), min(cut.stop, here.stop)
            if a < b:
                kept[:, a - cut.start : b - cut.start] = ab[:, a - here.start : b - here.start]
    for copy in copies:
        copy.wait()


def last_kernel(cut, above, late, before, out_in, out, held, sem):
    del out_in
    width = above.shape[0]
    top = above[...]
    change = dot(late[0], top)
    held[:width] = before[:width] + (top - change[:width])
    held[width:] = before[width:] - change[width:]
    copy = pltpu.make_async_copy(held, out.at[pl.ds(0, 2 * width), cut], sem)
    copy.start()
    copy.wait()


def smem():
    return pl.BlockSpec(memory_space=pltpu.SMEM)


def hbm():
    return pl.BlockSpec(memory_space=pltpu.HBM)


def whole(shape, index=None):
    index = (0,) * len(shape) if index is None else index
    return pl.BlockSpec(shape, lambda tile: index)


def columns(rows, span, row=0):
    return pl.BlockSpec((rows, span), lambda tile: (row, tile))


def call(kernel, tiles, in_specs, out_specs, out_shape, operands, name, vmem=VMEM_LIMIT, **extra):
    shapes = [jax.ShapeDtypeStruct(shape, F32) for shape in out_shape]
    return pl.pallas_call(
        kernel,
        grid=(tiles,),
        in_specs=in_specs,
        out_specs=out_specs,
        out_shape=shapes,
        cost_estimate=pl.CostEstimate(flops=1, bytes_accessed=1, transcendentals=0),
        compiler_params=pltpu.CompilerParams(vmem_limit_bytes=vmem),
        name=name,
        **extra,
    )(*operands)


def local(panel, inner_vecs, inner_factor, border_vecs, border_factor, group_start, group_span):
    width = inner_factor.shape[-1]
    height, cols = panel.shape
    steps = inner_factor.shape[1]
    span = cols // TILES
    own_i, own_b = inner_vecs[0], border_vecs[0]
    fac_i, fac_b = inner_factor[0], border_factor[0]

    below = from_behind(panel[:width], "row", -1)
    own_early, fac_early = own_i[:2], fac_i[:2]
    other_early = other_core(own_early)
    other_late = other_core(own_i[2:])
    other_b = other_core(own_b)

    square = (2 * width, 2 * width)
    vec = (steps, width, width)
    ups = [part.stop - part.start for part in pieces(cols, EIGHTHS_UP)]
    cuts = pieces(cols, EIGHTHS_DOWN)
    downs = [cut.stop - cut.start for cut in cuts]
    extra = width * width // (lax.axis_size("col") * ups[-1])
    shapes = [(width, up) for up in ups[:-1]] + [(width + extra, ups[-1])]
    early, bc, *up_messages = call(
        first_kernel,
        1,
        [hbm(), whole((2, width, width)), hbm(), hbm()],
        [whole((2,) + square), whole((2 * width, cols))] + [whole(shape) for shape in shapes],
        [(2,) + square, (2 * width, cols)] + shapes,
        [own_early, other_early, fac_early, panel],
        "inner_and_up",
        vmem=50 * 1024 * 1024,
        scratch_shapes=[
            pltpu.VMEM((2, width, width), F32),
            pltpu.VMEM((2, width, width), F32),
            pltpu.VMEM((2 * width, cols), F32),
            pltpu.SemaphoreType.DMA((2 + len(ups),)),
        ],
    )
    from_below = [from_behind(message, "row", -1) for message in up_messages]
    below, from_below[0] = lax.optimization_barrier((below, from_below[0]))
    late, border = call(
        matrix_kernel,
        1,
        [whole((2, width, width), (1, 0, 0)), whole((2, width, width)), whole((2, width, width), (1, 0, 0))] + [whole(vec)] * 3,
        [whole((2,) + square), whole((steps,) + square)],
        [(2,) + square, (steps,) + square],
        [own_i, other_late, fac_i, own_b, other_b, fac_b],
        "matrices",
    )
    down_message, cd = call(
        second_kernel,
        TILES,
        [smem(), smem(), columns(width, span, 3), columns(width, span), columns(width, span, 1), whole((2,) + square)],
        [columns(width, span), columns(2 * width, span)],
        [(width, cols), (2 * width, cols)],
        [group_start, group_span, panel, below, bc, border],
        "border_and_down",
    )
    above = from_behind(down_message, "row", 1)
    d, *sent = call(
        third_kernel,
        1,
        [smem(), smem(), whole((width, cols)), whole((2 * width, cols)), whole((1,) + square, (2, 0, 0)), whole((extra, ups[-1]))] + [whole(shape) for shape in shapes],
        [whole((width, cols))] + [whole((width, down)) for down in downs],
        [(width, cols)] + [(width, down) for down in downs],
        [group_start, group_span, down_message, cd, border, other_core(from_below[-1][width:])] + from_below,
        "second_border",
    )
    last = [from_behind(part, "row", 1) for part in sent]
    out, *before = call(
        fourth_kernel,
        1,
        [smem(), smem(), whole((width, cols)), whole((width, cols)), whole((2 * width, cols)), whole((2 * width, cols)), whole((width, cols)), whole((1,) + square, (1, 0, 0)), whole((2,) + square), whole((1,) + square, (3, 0, 0))],
        [pl.BlockSpec(memory_space=pl.ANY)] + [whole((2 * width, down)) for down in downs],
        [(height, cols)] + [(2 * width, down) for down in downs],
        [group_start, group_span, panel, above, bc, cd, d, early, late, border],
        "rest",
        scratch_shapes=[pltpu.VMEM((2 * width, cols), F32), pltpu.SemaphoreType.DMA((TILES,))],
    )
    for cut, down, part, kept in zip(cuts, downs, last, before):
        (out,) = call(
            functools.partial(last_kernel, cut),
            1,
            [whole((width, down)), whole((1, 2 * width, width), (1, 0, 0)), whole((2 * width, down)), pl.BlockSpec(memory_space=pl.ANY)],
            [pl.BlockSpec(memory_space=pl.ANY)],
            [(height, cols)],
            [part, late, kept, out],
            "finish",
            scratch_shapes=[pltpu.VMEM((2 * width, down), F32), pltpu.SemaphoreType.DMA],
            input_output_aliases={3: 0},
        )
    return out


def solution(mesh):
    placed = (
        P("row", "col"),
        P("row", None, "col", None),
        P("row", None, None, None),
        P("row", None, "col", None),
        P("row", None, None, None),
        P(),
        P(),
    )
    return jax.shard_map(
        local, mesh=mesh, in_specs=placed, out_specs=P("row", "col"), check_vma=False
    )
```

```python
import functools

import jax
import jax.numpy as jnp
from jax import lax
from jax.experimental import pallas as pl
from jax.experimental.pallas import tpu as pltpu
from jax.sharding import PartitionSpec as P

F32 = jnp.float32
TILES = 2
EIGHTHS_UP = (4, 4)
EIGHTHS_DOWN = (6, 2)
VMEM_LIMIT = 24 * 1024 * 1024


def from_behind(value, axis, by):
    devices = lax.axis_size(axis)
    pairs = [(i, i + by) for i in range(devices) if 0 <= i + by < devices]
    return lax.ppermute(value, axis, pairs)


def other_core(value):
    cores = lax.axis_size("col")
    return lax.ppermute(value, "col", [(i, (i + 1) % cores) for i in range(cores)])


def split(x):
    high = x.astype(jnp.bfloat16)
    return high, (x - high.astype(F32)).astype(jnp.bfloat16)


def dot(x, y, contract=(1, 0)):
    def product(left, right):
        return lax.dot_general(
            left,
            right,
            (((contract[0],), (contract[1],)), ((), ())),
            preferred_element_type=F32,
        )

    xh, xl = split(x)
    yh, yl = split(y)
    return product(xl, yh) + product(xh, yl) + product(xh, yh)


def exact_dot(x, y):
    return jnp.dot(x, y, precision=lax.Precision.HIGHEST, preferred_element_type=F32)


def change_of(first, second, factor, core):
    upper = jnp.where(core == 0, first, second)
    lower = jnp.where(core == 0, second, first)
    vectors = jnp.concatenate([upper, lower], axis=0)
    return dot(dot(vectors, factor), vectors, (1, 1))


def stacked(upper, lower):
    return jnp.concatenate([upper, lower], axis=0)


def unpacked(rows, width):
    return jnp.concatenate(
        [rows[:, at : at + width] for at in range(0, rows.shape[1], width)], axis=0
    )


def ordered(mine, other):
    core = lax.axis_index("col")
    return stacked(jnp.where(core == 0, mine, other), jnp.where(core == 0, other, mine))


def is_active(starts, spans, step):
    index = lax.axis_index("row")
    return (index >= starts[step]) & (index < starts[step] + spans[step])


def pieces(cols, eighths):
    ends = [cols * sum(eighths[:at]) // 8 for at in range(len(eighths) + 1)]
    return [slice(a, b) for a, b in zip(ends[:-1], ends[1:])]


def first_kernel(own, other, factor, panel, early, bc, *rest):
    *messages, vectors, factors, band, sems = rest
    width = factor.shape[-1]
    parts = pieces(panel.shape[1], EIGHTHS_UP)
    copies = [
        pltpu.make_async_copy(own.at[pl.ds(0, 2)], vectors, sems.at[0]),
        pltpu.make_async_copy(factor.at[pl.ds(0, 2)], factors, sems.at[1]),
    ] + [
        pltpu.make_async_copy(
            panel.at[pl.ds(width, 2 * width), part], band.at[:, part], sems.at[2 + at]
        )
        for at, part in enumerate(parts)
    ]
    for copy in copies:
        copy.start()
    copies[0].wait()
    copies[1].wait()
    core = lax.axis_index("col")
    for step in range(2):
        early[step] = change_of(vectors[step], other[step], factors[step], core)
    last = messages[-1]
    extra = last.shape[0] - width
    half = jnp.where(core == 0, early[1, : width // 2, :width], early[1, width // 2 : width, :width])
    for block in range(last.shape[1] // width):
        last[width:, block * width : (block + 1) * width] = half[
            block * extra : (block + 1) * extra
        ]
    for at, part in enumerate(parts):
        copies[2 + at].wait()
        tall = band[:, part]
        tall = tall - dot(early[0], tall)
        bc[:, part] = tall
        messages[at][:width] = dot(early[1, :width, width:], tall[:width])


def matrix_kernel(own_i, other_i, fac_i, own_b, other_b, fac_b, late, border):
    core = lax.axis_index("col")
    for step in range(late.shape[0]):
        late[step] = change_of(own_i[step], other_i[step], fac_i[step], core)
    for step in range(border.shape[0]):
        border[step] = change_of(own_b[step], other_b[step], fac_b[step], core)


def second_kernel(starts, spans, d, below, c, border, message, cd):
    width = d.shape[0]
    band = stacked(d[...], below[...])
    band = jnp.where(is_active(starts, spans, 0), band - dot(border[0], band), band)
    message[...] = band[width:]
    band = stacked(c[...], band[:width])
    cd[...] = jnp.where(is_active(starts, spans, 1), band - exact_dot(border[1], band), band)


def third_kernel(starts, spans, below, cd, border, half, *rest):
    count = len(EIGHTHS_UP)
    messages, d_out, sent = rest[:count], rest[count], rest[count + 1 :]
    width, cols = d_out.shape
    cuts = pieces(cols, EIGHTHS_DOWN)
    mixing = ordered(unpacked(messages[-1][width:], width), unpacked(half[...], width))
    for message, part in zip(messages, pieces(cols, EIGHTHS_UP)):
        low = below[:, part]
        low = low - dot(mixing, low) - message[:width]
        band = stacked(cd[width:, part], low)
        band = jnp.where(is_active(starts, spans, 2), band - dot(border[0], band), band)
        d_out[:, part] = band[:width]
        for cut, out in zip(cuts, sent):
            a, b = max(cut.start, part.start), min(cut.stop, part.stop)
            if a < b:
                out[:, a - cut.start : b - cut.start] = band[
                    width:, a - part.start : b - part.start
                ]


def fourth_kernel(starts, spans, raw, above, bc, cd, d, second, late, border, out, *rest):
    *before, held, sems = rest
    width, cols = raw.shape
    span = cols // TILES
    first = lax.axis_index("row") == 0
    copies = []
    for part in range(TILES):
        here = slice(part * span, (part + 1) * span)
        ab = stacked(jnp.where(first, raw[:, here], above[:, here]), bc[:width, here])
        ab = ab - dot(second[0], ab)
        low = stacked(ab[width:], cd[:width, here])
        low = low - dot(late[0], low)
        end = stacked(low[width:], d[:, here])
        held[:, here] = jnp.where(is_active(starts, spans, 3), end - dot(border[0], end), end)
        copy = pltpu.make_async_copy(
            held.at[:, pl.ds(part * span, span)],
            out.at[pl.ds(2 * width, 2 * width), pl.ds(part * span, span)],
            sems.at[part],
        )
        copy.start()
        copies.append(copy)
        ab = stacked(jnp.where(first, ab[:width], 0.0), low[:width])
        ab = ab - dot(late[1], ab)
        for cut, kept in zip(pieces(cols, EIGHTHS_DOWN), before):
            a, b = max(cut.start, here.start), min(cut.stop, here.stop)
            if a < b:
                kept[:, a - cut.start : b - cut.start] = ab[:, a - here.start : b - here.start]
    for copy in copies:
        copy.wait()


def last_kernel(cut, above, late, before, out_in, out, held, sem):
    del out_in
    width = above.shape[0]
    top = above[...]
    change = dot(late[0], top)
    held[:width] = before[:width] + (top - change[:width])
    held[width:] = before[width:] - change[width:]
    copy = pltpu.make_async_copy(held, out.at[pl.ds(0, 2 * width), cut], sem)
    copy.start()
    copy.wait()


def smem():
    return pl.BlockSpec(memory_space=pltpu.SMEM)


def hbm():
    return pl.BlockSpec(memory_space=pltpu.HBM)


def whole(shape, index=None):
    index = (0,) * len(shape) if index is None else index
    return pl.BlockSpec(shape, lambda tile: index)


def columns(rows, span, row=0):
    return pl.BlockSpec((rows, span), lambda tile: (row, tile))


def call(kernel, tiles, in_specs, out_specs, out_shape, operands, name, vmem=VMEM_LIMIT, **extra):
    shapes = [jax.ShapeDtypeStruct(shape, F32) for shape in out_shape]
    return pl.pallas_call(
        kernel,
        grid=(tiles,),
        in_specs=in_specs,
        out_specs=out_specs,
        out_shape=shapes,
        cost_estimate=pl.CostEstimate(flops=1, bytes_accessed=1, transcendentals=0),
        compiler_params=pltpu.CompilerParams(vmem_limit_bytes=vmem),
        name=name,
        **extra,
    )(*operands)


def local(panel, inner_vecs, inner_factor, border_vecs, border_factor, group_start, group_span):
    width = inner_factor.shape[-1]
    height, cols = panel.shape
    steps = inner_factor.shape[1]
    span = cols // TILES
    own_i, own_b = inner_vecs[0], border_vecs[0]
    fac_i, fac_b = inner_factor[0], border_factor[0]

    below = from_behind(panel[:width], "row", -1)
    own_early, fac_early = own_i[:2], fac_i[:2]
    other_early = other_core(own_early)
    other_late = other_core(own_i[2:])
    other_b = other_core(own_b)

    square = (2 * width, 2 * width)
    vec = (steps, width, width)
    ups = [part.stop - part.start for part in pieces(cols, EIGHTHS_UP)]
    cuts = pieces(cols, EIGHTHS_DOWN)
    downs = [cut.stop - cut.start for cut in cuts]
    extra = width * width // (lax.axis_size("col") * ups[-1])
    shapes = [(width, up) for up in ups[:-1]] + [(width + extra, ups[-1])]
    early, bc, *up_messages = call(
        first_kernel,
        1,
        [hbm(), whole((2, width, width)), hbm(), hbm()],
        [whole((2,) + square), whole((2 * width, cols))] + [whole(shape) for shape in shapes],
        [(2,) + square, (2 * width, cols)] + shapes,
        [own_early, other_early, fac_early, panel],
        "inner_and_up",
        vmem=50 * 1024 * 1024,
        scratch_shapes=[
            pltpu.VMEM((2, width, width), F32),
            pltpu.VMEM((2, width, width), F32),
            pltpu.VMEM((2 * width, cols), F32),
            pltpu.SemaphoreType.DMA((2 + len(ups),)),
        ],
    )
    from_below = [from_behind(message, "row", -1) for message in up_messages]
    below, from_below[0] = lax.optimization_barrier((below, from_below[0]))
    late, border = call(
        matrix_kernel,
        1,
        [whole((2, width, width), (1, 0, 0)), whole((2, width, width)), whole((2, width, width), (1, 0, 0))] + [whole(vec)] * 3,
        [whole((2,) + square), whole((steps,) + square)],
        [(2,) + square, (steps,) + square],
        [own_i, other_late, fac_i, own_b, other_b, fac_b],
        "matrices",
    )
    down_message, cd = call(
        second_kernel,
        TILES,
        [smem(), smem(), columns(width, span, 3), columns(width, span), columns(width, span, 1), whole((2,) + square)],
        [columns(width, span), columns(2 * width, span)],
        [(width, cols), (2 * width, cols)],
        [group_start, group_span, panel, below, bc, border],
        "border_and_down",
    )
    above = from_behind(down_message, "row", 1)
    d, *sent = call(
        third_kernel,
        1,
        [smem(), smem(), whole((width, cols)), whole((2 * width, cols)), whole((1,) + square, (2, 0, 0)), whole((extra, ups[-1]))] + [whole(shape) for shape in shapes],
        [whole((width, cols))] + [whole((width, down)) for down in downs],
        [(width, cols)] + [(width, down) for down in downs],
        [group_start, group_span, down_message, cd, border, other_core(from_below[-1][width:])] + from_below,
        "second_border",
    )
    last = [from_behind(part, "row", 1) for part in sent]
    out, *before = call(
        fourth_kernel,
        1,
        [smem(), smem(), whole((width, cols)), whole((width, cols)), whole((2 * width, cols)), whole((2 * width, cols)), whole((width, cols)), whole((1,) + square, (1, 0, 0)), whole((2,) + square), whole((1,) + square, (3, 0, 0))],
        [pl.BlockSpec(memory_space=pl.ANY)] + [whole((2 * width, down)) for down in downs],
        [(height, cols)] + [(2 * width, down) for down in downs],
        [group_start, group_span, panel, above, bc, cd, d, early, late, border],
        "rest",
        scratch_shapes=[pltpu.VMEM((2 * width, cols), F32), pltpu.SemaphoreType.DMA((TILES,))],
    )
    for cut, down, part, kept in zip(cuts, downs, last, before):
        (out,) = call(
            functools.partial(last_kernel, cut),
            1,
            [whole((width, down)), whole((1, 2 * width, width), (1, 0, 0)), whole((2 * width, down)), pl.BlockSpec(memory_space=pl.ANY)],
            [pl.BlockSpec(memory_space=pl.ANY)],
            [(height, cols)],
            [part, late, kept, out],
            "finish",
            scratch_shapes=[pltpu.VMEM((2 * width, down), F32), pltpu.SemaphoreType.DMA],
            input_output_aliases={3: 0},
        )
    return out


def solution(mesh):
    placed = (
        P("row", "col"),
        P("row", None, "col", None),
        P("row", None, None, None),
        P("row", None, "col", None),
        P("row", None, None, None),
        P(),
        P(),
    )
    return jax.shard_map(
        local, mesh=mesh, in_specs=placed, out_specs=P("row", "col"), check_vma=False
    )
```

```python
import functools

import jax
import jax.numpy as jnp
from jax import lax
from jax.experimental import pallas as pl
from jax.experimental.pallas import tpu as pltpu
from jax.sharding import PartitionSpec as P

F32 = jnp.float32
TILES = 2
CHUNK = 256
EIGHTHS_UP = (4, 4)
EIGHTHS_DOWN = (6, 2)
VMEM_LIMIT = 24 * 1024 * 1024


def from_behind(value, axis, by):
    devices = lax.axis_size(axis)
    pairs = [(i, i + by) for i in range(devices) if 0 <= i + by < devices]
    return lax.ppermute(value, axis, pairs)


def other_core(value):
    cores = lax.axis_size("col")
    return lax.ppermute(value, "col", [(i, (i + 1) % cores) for i in range(cores)])


def split(x):
    high = x.astype(jnp.bfloat16)
    return high, (x - high.astype(F32)).astype(jnp.bfloat16)


def dot(x, y, contract=(1, 0)):
    xh, xl = split(x)
    yh, yl = split(y)
    return lax.dot_general(
        jnp.concatenate([xl, xh, xh], axis=contract[0]),
        jnp.concatenate([yh, yl, yh], axis=contract[1]),
        (((contract[0],), (contract[1],)), ((), ())),
        preferred_element_type=F32,
    )


def exact_dot(x, y):
    return jnp.dot(x, y, precision=lax.Precision.HIGHEST, preferred_element_type=F32)


def change_of(first, second, factor, core):
    upper = jnp.where(core == 0, first, second)
    lower = jnp.where(core == 0, second, first)
    vectors = jnp.concatenate([upper, lower], axis=0)
    return dot(dot(vectors, factor), vectors, (1, 1))


def stacked(upper, lower):
    return jnp.concatenate([upper, lower], axis=0)


def unpacked(rows, width):
    return jnp.concatenate(
        [rows[:, at : at + width] for at in range(0, rows.shape[1], width)], axis=0
    )


def ordered(mine, other):
    core = lax.axis_index("col")
    return stacked(jnp.where(core == 0, mine, other), jnp.where(core == 0, other, mine))


def is_active(starts, spans, step):
    index = lax.axis_index("row")
    return (index >= starts[step]) & (index < starts[step] + spans[step])


def pieces(cols, eighths):
    ends = [cols * sum(eighths[:at]) // 8 for at in range(len(eighths) + 1)]
    return [slice(a, b) for a, b in zip(ends[:-1], ends[1:])]


def first_kernel(own, other, factor, panel, early, bc, *rest):
    *messages, vectors, factors, band, sems = rest
    width = factor.shape[-1]
    parts = pieces(panel.shape[1], EIGHTHS_UP)
    copies = [
        pltpu.make_async_copy(own.at[pl.ds(0, 2)], vectors, sems.at[0]),
        pltpu.make_async_copy(factor.at[pl.ds(0, 2)], factors, sems.at[1]),
    ] + [
        pltpu.make_async_copy(
            panel.at[pl.ds(width, 2 * width), part], band.at[:, part], sems.at[2 + at]
        )
        for at, part in enumerate(parts)
    ]
    for copy in copies:
        copy.start()
    copies[0].wait()
    copies[1].wait()
    core = lax.axis_index("col")
    for step in range(2):
        early[step] = change_of(vectors[step], other[step], factors[step], core)
    last = messages[-1]
    extra = last.shape[0] - width
    half = jnp.where(core == 0, early[1, : width // 2, :width], early[1, width // 2 : width, :width])
    for block in range(last.shape[1] // width):
        last[width:, block * width : (block + 1) * width] = half[
            block * extra : (block + 1) * extra
        ]
    for at, part in enumerate(parts):
        copies[2 + at].wait()
        tall = band[:, part]
        tall = tall - dot(early[0], tall)
        bc[:, part] = tall
        messages[at][:width] = dot(early[1, :width, width:], tall[:width])


def matrix_kernel(own_i, other_i, fac_i, own_b, other_b, fac_b, late, border):
    core = lax.axis_index("col")
    for step in range(late.shape[0]):
        late[step] = change_of(own_i[step], other_i[step], fac_i[step], core)
    for step in range(border.shape[0]):
        border[step] = change_of(own_b[step], other_b[step], fac_b[step], core)


def second_kernel(starts, spans, d, below, c, border, message, cd):
    width = d.shape[0]
    band = stacked(d[...], below[...])
    band = jnp.where(is_active(starts, spans, 0), band - dot(border[0], band), band)
    message[...] = band[width:]
    band = stacked(c[...], band[:width])
    cd[...] = jnp.where(is_active(starts, spans, 1), band - exact_dot(border[1], band), band)


def third_kernel(starts, spans, below, cd, border, half, *rest):
    count = len(EIGHTHS_UP)
    messages, d_out, sent = rest[:count], rest[count], rest[count + 1 :]
    width, cols = d_out.shape
    cuts = pieces(cols, EIGHTHS_DOWN)
    mixing = ordered(unpacked(messages[-1][width:], width), unpacked(half[...], width))
    for message, part in zip(messages, pieces(cols, EIGHTHS_UP)):
        low = below[:, part]
        low = low - dot(mixing, low) - message[:width]
        band = stacked(cd[width:, part], low)
        band = jnp.where(is_active(starts, spans, 2), band - dot(border[0], band), band)
        d_out[:, part] = band[:width]
        for cut, out in zip(cuts, sent):
            a, b = max(cut.start, part.start), min(cut.stop, part.stop)
            if a < b:
                out[:, a - cut.start : b - cut.start] = band[
                    width:, a - part.start : b - part.start
                ]


def fourth_kernel(starts, spans, raw, above, bc, cd, d, second, late, border, out, *rest):
    *before, held, sems = rest
    width, cols = raw.shape
    span = cols // TILES
    first = lax.axis_index("row") == 0
    copies = []
    for part in range(TILES):
        here = slice(part * span, (part + 1) * span)
        ab = stacked(jnp.where(first, raw[:, here], above[:, here]), bc[:width, here])
        ab = ab - dot(second[0], ab)
        low = stacked(ab[width:], cd[:width, here])
        low = low - dot(late[0], low)
        end = stacked(low[width:], d[:, here])
        held[:, here] = jnp.where(is_active(starts, spans, 3), end - dot(border[0], end), end)
        copy = pltpu.make_async_copy(
            held.at[:, pl.ds(part * span, span)],
            out.at[pl.ds(2 * width, 2 * width), pl.ds(part * span, span)],
            sems.at[part],
        )
        copy.start()
        copies.append(copy)
        ab = stacked(jnp.where(first, ab[:width], 0.0), low[:width])
        ab = ab - dot(late[1], ab)
        for cut, kept in zip(pieces(cols, EIGHTHS_DOWN), before):
            a, b = max(cut.start, here.start), min(cut.stop, here.stop)
            if a < b:
                kept[:, a - cut.start : b - cut.start] = ab[:, a - here.start : b - here.start]
    for copy in copies:
        copy.wait()


def last_kernel(cut, above, late, before, out_in, out, held, sems):
    del out_in
    width, span = above.shape
    high, low = split(late[0])
    matrix = jnp.concatenate([low, high, high], axis=1)
    copies = []
    for at in range(span // CHUNK):
        here = slice(at * CHUNK, (at + 1) * CHUNK)
        top = above[:, here]
        high, low = split(top)
        change = jnp.dot(
            matrix, jnp.concatenate([high, low, high], axis=0), preferred_element_type=F32
        )
        held[:width, here] = before[:width, here] + (top - change[:width])
        held[width:, here] = before[width:, here] - change[width:]
        copy = pltpu.make_async_copy(
            held.at[:, here],
            out.at[pl.ds(0, 2 * width), pl.ds(cut.start + at * CHUNK, CHUNK)],
            sems.at[at],
        )
        copy.start()
        copies.append(copy)
    for copy in copies:
        copy.wait()


def smem():
    return pl.BlockSpec(memory_space=pltpu.SMEM)


def hbm():
    return pl.BlockSpec(memory_space=pltpu.HBM)


def whole(shape, index=None):
    index = (0,) * len(shape) if index is None else index
    return pl.BlockSpec(shape, lambda tile: index)


def columns(rows, span, row=0):
    return pl.BlockSpec((rows, span), lambda tile: (row, tile))


def call(kernel, tiles, in_specs, out_specs, out_shape, operands, name, vmem=VMEM_LIMIT, **extra):
    shapes = [jax.ShapeDtypeStruct(shape, F32) for shape in out_shape]
    return pl.pallas_call(
        kernel,
        grid=(tiles,),
        in_specs=in_specs,
        out_specs=out_specs,
        out_shape=shapes,
        cost_estimate=pl.CostEstimate(flops=1, bytes_accessed=1, transcendentals=0),
        compiler_params=pltpu.CompilerParams(vmem_limit_bytes=vmem),
        name=name,
        **extra,
    )(*operands)


def local(panel, inner_vecs, inner_factor, border_vecs, border_factor, group_start, group_span):
    width = inner_factor.shape[-1]
    height, cols = panel.shape
    steps = inner_factor.shape[1]
    span = cols // TILES
    own_i, own_b = inner_vecs[0], border_vecs[0]
    fac_i, fac_b = inner_factor[0], border_factor[0]

    below = from_behind(panel[:width], "row", -1)
    own_early, fac_early = own_i[:2], fac_i[:2]
    other_early = other_core(own_early)
    other_late = other_core(own_i[2:])
    other_b = other_core(own_b)

    square = (2 * width, 2 * width)
    vec = (steps, width, width)
    ups = [part.stop - part.start for part in pieces(cols, EIGHTHS_UP)]
    cuts = pieces(cols, EIGHTHS_DOWN)
    downs = [cut.stop - cut.start for cut in cuts]
    extra = width * width // (lax.axis_size("col") * ups[-1])
    shapes = [(width, up) for up in ups[:-1]] + [(width + extra, ups[-1])]
    early, bc, *up_messages = call(
        first_kernel,
        1,
        [hbm(), whole((2, width, width)), hbm(), hbm()],
        [whole((2,) + square), whole((2 * width, cols))] + [whole(shape) for shape in shapes],
        [(2,) + square, (2 * width, cols)] + shapes,
        [own_early, other_early, fac_early, panel],
        "inner_and_up",
        vmem=50 * 1024 * 1024,
        scratch_shapes=[
            pltpu.VMEM((2, width, width), F32),
            pltpu.VMEM((2, width, width), F32),
            pltpu.VMEM((2 * width, cols), F32),
            pltpu.SemaphoreType.DMA((2 + len(ups),)),
        ],
    )
    from_below = [from_behind(message, "row", -1) for message in up_messages]
    below, from_below[0] = lax.optimization_barrier((below, from_below[0]))
    late, border = call(
        matrix_kernel,
        1,
        [whole((2, width, width), (1, 0, 0)), whole((2, width, width)), whole((2, width, width), (1, 0, 0))] + [whole(vec)] * 3,
        [whole((2,) + square), whole((steps,) + square)],
        [(2,) + square, (steps,) + square],
        [own_i, other_late, fac_i, own_b, other_b, fac_b],
        "matrices",
    )
    down_message, cd = call(
        second_kernel,
        TILES,
        [smem(), smem(), columns(width, span, 3), columns(width, span), columns(width, span, 1), whole((2,) + square)],
        [columns(width, span), columns(2 * width, span)],
        [(width, cols), (2 * width, cols)],
        [group_start, group_span, panel, below, bc, border],
        "border_and_down",
    )
    above = from_behind(down_message, "row", 1)
    d, *sent = call(
        third_kernel,
        1,
        [smem(), smem(), whole((width, cols)), whole((2 * width, cols)), whole((1,) + square, (2, 0, 0)), whole((extra, ups[-1]))] + [whole(shape) for shape in shapes],
        [whole((width, cols))] + [whole((width, down)) for down in downs],
        [(width, cols)] + [(width, down) for down in downs],
        [group_start, group_span, down_message, cd, border, other_core(from_below[-1][width:])] + from_below,
        "second_border",
    )
    last = [from_behind(part, "row", 1) for part in sent]
    out, *before = call(
        fourth_kernel,
        1,
        [smem(), smem(), whole((width, cols)), whole((width, cols)), whole((2 * width, cols)), whole((2 * width, cols)), whole((width, cols)), whole((1,) + square, (1, 0, 0)), whole((2,) + square), whole((1,) + square, (3, 0, 0))],
        [pl.BlockSpec(memory_space=pl.ANY)] + [whole((2 * width, down)) for down in downs],
        [(height, cols)] + [(2 * width, down) for down in downs],
        [group_start, group_span, panel, above, bc, cd, d, early, late, border],
        "rest",
        scratch_shapes=[pltpu.VMEM((2 * width, cols), F32), pltpu.SemaphoreType.DMA((TILES,))],
    )
    for cut, down, part, kept in zip(cuts, downs, last, before):
        (out,) = call(
            functools.partial(last_kernel, cut),
            1,
            [whole((width, down)), whole((1, 2 * width, width), (1, 0, 0)), whole((2 * width, down)), pl.BlockSpec(memory_space=pl.ANY)],
            [pl.BlockSpec(memory_space=pl.ANY)],
            [(height, cols)],
            [part, late, kept, out],
            "finish",
            scratch_shapes=[
                pltpu.VMEM((2 * width, down), F32),
                pltpu.SemaphoreType.DMA((down // CHUNK,)),
            ],
            input_output_aliases={3: 0},
        )
    return out


def solution(mesh):
    placed = (
        P("row", "col"),
        P("row", None, "col", None),
        P("row", None, None, None),
        P("row", None, "col", None),
        P("row", None, None, None),
        P(),
        P(),
    )
    return jax.shard_map(
        local, mesh=mesh, in_specs=placed, out_specs=P("row", "col"), check_vma=False
    )
```
